256 devices in a mesh: tm: 16 (over y, x), space: 16 (over z, core).
Axes of the slice: x: 4, y: 4, z: 8, core: 2. Of those that a mesh axis runs over, the one named last changes fastest.
Arguments:
- base_start: float32 [16, 512, 4096], P('tm', 'space'), may hold values from -6 to 6
- direction: float32 [16, 512, 4096], P('tm', 'space'), may hold values from -6 to 6
- damp_levels: int32 [64, 32], P('space'), may hold values from 0 to 3
- damp_table: float32 [4], replicated, may hold values from 0.1 to 2
Outputs:
- product: float32 [16, 512, 4096], P('tm', 'space')
The draws below stay inside these ranges and needn't reach their ends.
All inputs are finite; a program needn't handle non-finite values.
Results may differ from the reference program's by a relative error of at most 0.00002.
Values sent between devices are 32-bit elements; how exact they have to be, the bound alone decides.
A program may use at most 64 MiB of HBM per device.

```python
import math
import jax
import jax.numpy as jnp
from jax import lax

NX = 4096
STEPS = 4
LEVELS = 4
NY = 512
SEGS = 16


def touch_ends(result, rng, low, high):
    longest = result.shape.index(max(result.shape))
    spots = []
    for shift in (0, 1):
        where = [jax.random.randint(jax.random.fold_in(rng, axis), (), 0, length) for axis, length in enumerate(result.shape)]
        where[longest] = (where[longest] + shift) % result.shape[longest]
        spots.append(tuple(where))
    return result.at[spots[0]].set(low).at[spots[1]].set(high)


def steps_of(own_key, dims, cuts, least, high):
    level, own = 1.0, jax.random.fold_in(own_key, 6)
    for position, blocks in cuts:
        steps = jnp.exp(jax.random.uniform(jax.random.fold_in(own, position), (blocks,), jnp.float32, least / len(cuts), high / len(cuts)))
        level = level * jnp.repeat(steps, dims[position] // blocks).reshape([-1 if axis == position else 1 for axis in range(len(dims))])
    return level


def gaussian(stream_key, extent, width, reach, pieces=(), held_as=jnp.bfloat16):
    result = width * jax.random.normal(stream_key, extent, jnp.float32)
    if pieces:
        result = result * steps_of(stream_key, extent, pieces, -0.22, 0.18)
    return jnp.clip(result, -reach, reach).astype(held_as)


def setup_inputs(seed: int = 0) -> dict:
    splits = jax.random.split(jax.random.key(seed), 5)
    return {
        "base_start": gaussian(splits[0], (SEGS, NY, NX), 1.0, 6.0, ((0, 16), (1, 16)), jnp.float32),
        "direction": gaussian(splits[1], (SEGS, NY, NX), 1.0, 6.0, ((0, 16), (1, 16)), jnp.float32),
        "damp_levels": touch_ends(jax.random.randint(splits[2], (NY // 8, NX // 128), 0, LEVELS), jax.random.fold_in(splits[2], 1), 0, LEVELS - 1).astype(jnp.int32),
        "damp_table": jnp.clip(jnp.exp(jax.random.uniform(splits[3], (LEVELS,), jnp.float32, math.log(0.1), math.log(2.0))), 0.1, 2.0),
    }


coef_lap = 0.05
coef_bih = 0.028
coef_slope = 0.05


def shave(field, depth):
    return field[..., depth:field.shape[-2] - depth, :]


def laplace(padded):
    center = padded[..., 1:-1, :]
    return padded[..., 2:, :] + padded[..., :-2, :] + jnp.roll(center, 1, -1) + jnp.roll(center, -1, -1) - 4.0 * center


def slope_cols(padded):
    center = padded[..., 1:-1, :]
    return (jnp.roll(center, -1, -1) - jnp.roll(center, 1, -1)) * 0.5


def slope_rows(padded):
    return (padded[..., 2:, :] - padded[..., :-2, :]) * 0.5


def base_step(padded):
    first = laplace(padded)
    second = laplace(first)
    along_x = shave(slope_cols(padded), 1)
    along_y = shave(slope_rows(padded), 1)
    return shave(padded, 2) - coef_lap * shave(first, 1) - coef_bih * second - coef_slope * (along_x * along_x + along_y * along_y)


def tangent_step(base_pad, pert_pad):
    first = laplace(pert_pad)
    second = laplace(first)
    cross = shave(slope_cols(base_pad), 1) * shave(slope_cols(pert_pad), 1) + shave(slope_rows(base_pad), 1) * shave(slope_rows(pert_pad), 1)
    return shave(pert_pad, 2) - coef_lap * shave(first, 1) - coef_bih * second - 2.0 * coef_slope * cross


def adjoint_step(base_pad, dual_pad):
    first = laplace(dual_pad)
    second = laplace(first)
    inner = shave(dual_pad, 1)
    flux_x = slope_cols(base_pad) * inner
    flux_y = slope_rows(base_pad) * inner
    spread = slope_cols(flux_x) + slope_rows(flux_y)
    return shave(dual_pad, 2) - coef_lap * shave(first, 1) - coef_bih * second + 2.0 * coef_slope * spread


def wrap_rows(field):
    return jnp.concatenate([field[-2:], field, field[:2]], 0)


def reference(base_start, direction, damp_levels, damp_table):
    def forward(pair):
        state, pert = pair
        for step in range(STEPS):
            base_pad = wrap_rows(state)
            pert = tangent_step(base_pad, wrap_rows(pert))
            state = base_step(base_pad)
        return pert

    ends = lax.map(forward, (base_start, direction))
    resid = ends - jnp.roll(direction, -1, 0)

    def backward(pair):
        state, dual = pair
        stored = []
        for step in range(STEPS):
            base_pad = wrap_rows(state)
            stored.append(base_pad)
            state = base_step(base_pad)
        for step in range(STEPS - 1, -1, -1):
            dual = adjoint_step(stored[step], wrap_rows(dual))
        return dual

    back = lax.map(backward, (base_start, resid))
    levels = jnp.arange(LEVELS).astype(jnp.int32)
    coarse = jnp.sum(jnp.where(damp_levels[..., None] == levels, damp_table, jnp.zeros_like(damp_table)), -1)
    damp = jnp.repeat(jnp.repeat(coarse, 8, 0), 128, 1)
    return back - jnp.roll(resid, 1, 0) + damp[None] * direction
```

```python
import functools
import math

import jax
import jax.numpy as jnp
from jax import lax
from jax.experimental import pallas as pl
from jax.experimental.pallas import tpu as pltpu
from jax.sharding import PartitionSpec as P

MESH = pl.DeviceIdType.MESH

STEPS = 4
ROWS = 32
COLS = 4096
LANES = 128
CHUNKS = COLS // LANES
OFF = 16
HELD = ROWS + 2 * OFF

coef_lap = 0.05
coef_bih = 0.028
coef_slope = 0.05

_root = math.sqrt((coef_lap / coef_bih) ** 2 + 4.0 / coef_bih)
NEAR = 4.0 + (-coef_lap / coef_bih + _root) / 2.0
FAR = 4.0 + (-coef_lap / coef_bih - _root) / 2.0
SLOPE = coef_slope / (2.0 * coef_bih)
SCALE = coef_bih**STEPS


def beside(x):
    lane = lax.broadcasted_iota(jnp.int32, (1, 1, LANES), 2)
    right = pltpu.roll(x, LANES - 1, 2)
    left = pltpu.roll(x, 1, 2)
    right_next = jnp.concatenate([right[:, 8:], pltpu.roll(right[:, :8], 7, 1)], 1)
    left_next = jnp.concatenate([pltpu.roll(left[:, 24:], 1, 1), left[:, :24]], 1)
    return (
        jnp.where(lane == LANES - 1, right_next, right),
        jnp.where(lane == 0, left_next, left),
    )


def over_rows(low, high, most, body):
    count = high - low + 1
    steps = -(-count // most)
    size = -(-count // steps)

    def step(i, carry):
        for j in range(size):
            body(low + OFF + i * size + j)
        return carry

    if steps == 1:
        step(0, 0)
    else:
        lax.fori_loop(0, steps, step, 0)


def cross_of(ref, r):
    return ref[pl.ds(r, 1)], ref[pl.ds(r - 1, 1)], ref[pl.ds(r + 1, 1)]


def forward_first(k, b, low, high, most, base=True, tangent=True):
    state, half, grad_x, grad_y = b.state.at[k], b.state_half.at[k], b.grad_x.at[k], b.grad_y.at[k]
    pert, pert_half, cross = b.pert.at[k], b.pert_half.at[k], b.cross.at[k]

    def body(r):
        row = pl.ds(r, 1)
        c, n, s = cross_of(state, r)
        right, left = beside(c)
        slope_x, slope_y = right - left, s - n
        grad_x[row] = slope_x
        grad_y[row] = slope_y
        if base:
            half[row] = ((right + left) + (n + s)) - NEAR * c
        if tangent:
            c, n, s = cross_of(pert, r)
            right, left = beside(c)
            pert_half[row] = ((right + left) + (n + s)) - NEAR * c
            cross[row] = slope_x * (right - left) + slope_y * (s - n)

    over_rows(low, high, most, body)


def forward_second(k, b, low, high, most, base=True, tangent=True):
    half, grad_x, grad_y = b.state_half.at[k], b.grad_x.at[k], b.grad_y.at[k]
    pert_half, cross, pert_next = b.pert_half.at[k], b.cross.at[k], b.pert.at[k + 1]
    if base:
        state_next = b.state.at[k + 1]

    def body(r):
        row = pl.ds(r, 1)
        if base:
            c, n, s = cross_of(half, r)
            right, left = beside(c)
            slope_x, slope_y = grad_x[row], grad_y[row]
            linear = ((right + left) + (n + s)) - FAR * c
            squares = slope_x * slope_x + slope_y * slope_y
            state_next[row] = linear * (-coef_bih) + squares * (-coef_bih / 2.0)
        if tangent:
            c, n, s = cross_of(pert_half, r)
            right, left = beside(c)
            pert_next[row] = (((right + left) + (n + s)) - FAR * c) + cross[row]

    over_rows(low, high, most, body)


def adjoint_first(k, b, low, high, most):
    dual, grad_x, grad_y = b.dual.at[k + 1], b.grad_x.at[k], b.grad_y.at[k]
    half, flux_dx, flux_y = b.dual_half.at[k], b.flux_dx.at[k], b.flux_y.at[k]

    def body(r):
        row = pl.ds(r, 1)
        c, n, s = cross_of(dual, r)
        right, left = beside(c)
        half[row] = ((right + left) + (n + s)) - NEAR * c
        right, left = beside(grad_x[row] * c)
        flux_dx[row] = right - left
        flux_y[row] = grad_y[row] * c

    over_rows(low, high, most, body)


def adjoint_second(k, b, low, high, most):
    half, flux_dx, flux_y, dual_next = b.dual_half.at[k], b.flux_dx.at[k], b.flux_y.at[k], b.dual.at[k]

    def body(r):
        c, n, s = cross_of(half, r)
        right, left = beside(c)
        spread = flux_dx[pl.ds(r, 1)] + (flux_y[pl.ds(r + 1, 1)] - flux_y[pl.ds(r - 1, 1)])
        dual_next[pl.ds(r, 1)] = (((right + left) + (n + s)) - FAR * c) - spread

    over_rows(low, high, most, body)


def by_rows(count, body):
    lax.fori_loop(0, count, lambda i, carry: (body(i), carry)[1], 0)


def spread_tile(tile, dest, first, scale=None):
    def body(i):
        for q in range(4):
            part = tile[pl.ds(q * 8 + i, 8, 32), :]
            dest[OFF + first + i, q * 8 : q * 8 + 8, :] = part if scale is None else part * scale

    by_rows(8, body)


class Buffers:
    def __init__(self, names, refs):
        self.__dict__.update(zip(names, refs, strict=True))


def row_buffer(*lead):
    return pltpu.VMEM((*lead, CHUNKS, LANES), jnp.float32)


def tiles(*lead):
    return pltpu.VMEM((*lead, 8 * CHUNKS, LANES), jnp.float32)


ENDS = ((14, 4), (10, 4), (18, 4), (8, 2), (22, 2), (0, 8), (24, 8))
BACK = ((8, 4), (20, 4), (12, 8))

SCRATCH = {
    "base_in": tiles(4),
    "dir_in": tiles(4),
    "out_tiles": tiles(4),
    "halo_base": tiles(2, 2),
    "halo_dir": tiles(2),
    "next_tiles": tiles(2),
    "next_rows": row_buffer(HELD),
    "prev_ends": row_buffer(HELD),
    "state": row_buffer(STEPS, HELD),
    "state_half": row_buffer(STEPS, HELD),
    "grad_x": row_buffer(STEPS, HELD),
    "grad_y": row_buffer(STEPS, HELD),
    "pert": row_buffer(STEPS + 1, HELD),
    "pert_half": row_buffer(STEPS, HELD),
    "cross": row_buffer(STEPS, HELD),
    "dual": row_buffer(STEPS + 1, HELD),
    "dual_half": row_buffer(STEPS, HELD),
    "flux_dx": row_buffer(STEPS, HELD),
    "flux_y": row_buffer(STEPS, HELD),
    "damp": row_buffer(4),
    "levels": pltpu.VMEM((4, CHUNKS), jnp.int32),
    "table": pltpu.SMEM((4,), jnp.float32),
    "local_sem": pltpu.SemaphoreType.DMA((12,)),
    "halo_send": pltpu.SemaphoreType.DMA((6,)),
    "halo_recv": pltpu.SemaphoreType.DMA((6,)),
    "back_send": pltpu.SemaphoreType.DMA((2 + len(BACK),)),
    "back_recv": pltpu.SemaphoreType.DMA((2 + len(BACK),)),
    "dual_send": pltpu.SemaphoreType.DMA((2,)),
    "dual_recv": pltpu.SemaphoreType.DMA((2,)),
    "ends_send": pltpu.SemaphoreType.DMA((len(ENDS),)),
    "ends_recv": pltpu.SemaphoreType.DMA((len(ENDS),)),
}


def kernel(segments, slabs, base, direction, levels, table, product, *scratch):
    b = Buffers(SCRATCH, scratch)
    tm, sp = lax.axis_index("tm"), lax.axis_index("space")
    after, before = lax.rem(tm + 1, segments), lax.rem(tm + segments - 1, segments)
    below, above = lax.rem(sp + 1, slabs), lax.rem(sp + slabs - 1, slabs)
    next_dev, prev_dev, down_dev, up_dev = (after, sp), (before, sp), (tm, below), (tm, above)

    barrier = pltpu.get_barrier_semaphore()
    for dev in (next_dev, prev_dev, down_dev, up_dev):
        pl.semaphore_signal(barrier, inc=1, device_id=dev, device_id_type=MESH)

    load = [
        pltpu.make_async_copy(base, b.base_in, b.local_sem.at[0]),
        pltpu.make_async_copy(direction, b.dir_in, b.local_sem.at[1]),
        pltpu.make_async_copy(levels, b.levels, b.local_sem.at[2]),
        pltpu.make_async_copy(table, b.table, b.local_sem.at[3]),
    ]
    for copy in load:
        copy.start()

    def remote(src, dst, send, recv, dev):
        return pltpu.make_async_remote_copy(
            src_ref=src, dst_ref=dst, send_sem=send, recv_sem=recv, device_id=dev, device_id_type=MESH
        )

    halo = [
        remote(src, dst, b.halo_send.at[i], b.halo_recv.at[i], dev)
        for i, (src, dst, dev) in enumerate(
            [
                (base.at[3], b.halo_base.at[0, 0], down_dev),
                (base.at[0], b.halo_base.at[1, 0], up_dev),
                (direction.at[3], b.halo_dir.at[0], down_dev),
                (direction.at[0], b.halo_dir.at[1], up_dev),
                (base.at[2], b.halo_base.at[0, 1], down_dev),
                (base.at[1], b.halo_base.at[1, 1], up_dev),
            ]
        )
    ]
    back = [
        remote(direction.at[3 * i], b.next_tiles.at[i], b.back_send.at[i], b.back_recv.at[i], prev_dev)
        for i in range(2)
    ]
    for i, (first, count) in enumerate(BACK):
        rows = pl.ds(OFF + first, count)
        back.append(
            remote(
                b.pert.at[0, rows], b.next_rows.at[rows], b.back_send.at[2 + i], b.back_recv.at[2 + i], prev_dev
            )
        )
    ends = []
    for i, (first, count) in enumerate(ENDS):
        rows = pl.ds(OFF + first, count)
        ends.append(
            remote(b.pert.at[STEPS, rows], b.prev_ends.at[rows], b.ends_send.at[i], b.ends_recv.at[i], next_dev)
        )
    dual = [
        remote(
            b.dual.at[STEPS, pl.ds(OFF + src, 8)],
            b.dual.at[STEPS, pl.ds(OFF + dst, 8)],
            b.dual_send.at[i],
            b.dual_recv.at[i],
            dev,
        )
        for i, (src, dst, dev) in enumerate(((ROWS - 8, -8, down_dev), (0, ROWS, up_dev)))
    ]

    pl.semaphore_wait(barrier, 4)
    for copy in halo[:4]:
        copy.start()
    for copy in back[:2]:
        copy.start()
    for copy in halo[4:]:
        copy.start()

    load[1].wait()
    for t in range(4):
        spread_tile(b.dir_in.at[t], b.pert.at[0], 8 * t)
    for copy in back[2:]:
        copy.start()
    load[0].wait()
    for t in range(4):
        spread_tile(b.base_in.at[t], b.state.at[0], 8 * t, SLOPE)

    def strip(k, low, high, sides, most):
        first_low = low - 1 if sides <= 0 else low + 1
        first_high = high + 1 if sides >= 0 else high - 1
        forward_first(k, b, first_low, first_high, most, base=k < STEPS - 1)
        forward_second(k, b, low, high, most, base=k < STEPS - 1)

    for k in range(STEPS):
        reach = 2 * (STEPS - 1 - k)
        strip(k, 14 - reach, 17 + reach, 0, 32)
    ends[0].start()
    for k in range(STEPS):
        reach = 2 * (STEPS - 1 - k)
        strip(k, 10 - reach, 13 - reach, -1, 32)
        strip(k, 18 + reach, 21 + reach, 1, 32)
    ends[1].start()
    ends[2].start()
    for k in range(STEPS):
        reach = 2 * (STEPS - 1 - k)
        strip(k, 8 - reach, 9 - reach, -1, 32)
        strip(k, 22 + reach, 23 + reach, 1, 32)
    ends[3].start()
    ends[4].start()

    for copy in halo[:4]:
        copy.wait()
    for side, first in ((0, -8), (1, ROWS)):
        spread_tile(b.halo_base.at[side, 0], b.state.at[0], first, SLOPE)
        spread_tile(b.halo_dir.at[side], b.pert.at[0], first)
    for k in range(STEPS):
        strip(k, -6 + 2 * k, 1 + 2 * k, -1, 8)
        strip(k, 30 - 2 * k, 37 - 2 * k, 1, 8)
    ends[5].start()
    ends[6].start()

    for copy in halo[4:]:
        copy.wait()
    for side, first in ((0, -16), (1, ROWS + 8)):
        spread_tile(b.halo_base.at[side, 1], b.state.at[0], first, SLOPE)
    for k in range(STEPS):
        last = k == STEPS - 1
        forward_first(k, b, -15 + 2 * k, -8 + 2 * k, 8, base=not last, tangent=False)
        forward_first(k, b, 39 - 2 * k, 46 - 2 * k, 8, base=not last, tangent=False)
        if not last:
            forward_second(k, b, -14 + 2 * k, -7 + 2 * k, 8, tangent=False)
            forward_second(k, b, 38 - 2 * k, 45 - 2 * k, 8, tangent=False)

    load[2].wait()
    load[3].wait()
    held = b.levels[...]
    coarse = jnp.zeros(held.shape, jnp.float32)
    for level in range(4):
        coarse = coarse + jnp.where(held == level, b.table[level], 0.0)
    entry = lax.broadcasted_iota(jnp.int32, (CHUNKS, CHUNKS), 0)
    chunk = lax.broadcasted_iota(jnp.int32, (CHUNKS, CHUNKS), 1)
    own = chunk == 4 * (entry % 8) + entry // 8
    for t in range(4):
        value = jnp.sum(jnp.where(own, coarse[t : t + 1], 0.0), axis=1, keepdims=True)
        b.damp[t] = jnp.broadcast_to(value, (CHUNKS, LANES))

    def residual(first, count, source):
        def body(i):
            r = OFF + first + i
            b.dual[STEPS, r] = b.pert[STEPS, r] * SCALE - source(r, i)

        by_rows(count, body)

    for side in range(2):
        back[side].wait()
        spread_tile(b.next_tiles.at[side], b.next_rows, 24 * side)
        residual(24 * side, 8, lambda r, i: b.next_rows[r])
    dual[0].start()
    dual[1].start()
    for i in range(2):
        back[2 + i].wait()
        residual(*BACK[i], lambda r, i: b.next_rows[r])
    dual[0].wait()
    dual[1].wait()

    for k in range(STEPS - 1, -1, -1):
        far, near = -2 * k, 3 + 2 * k
        adjoint_first(k, b, far - 1, near + 1, 8)
        adjoint_first(k, b, 30 - near, 32 - far, 8)
        adjoint_second(k, b, far, near, 8)
        adjoint_second(k, b, 31 - near, 31 - far, 8)
    back[4].wait()
    residual(*BACK[2], lambda r, i: b.next_rows[r])
    for k in range(STEPS - 1, -1, -1):
        near = 3 + 2 * k
        adjoint_first(k, b, near + 2, 29 - near, 32)
        adjoint_second(k, b, near + 1, 30 - near, 32)

    def finish(t):
        def body(i):
            r = OFF + 8 * t + i
            value = (b.dual[0, r] - b.prev_ends[r]) * SCALE + (1.0 + b.damp[t]) * b.pert[0, r]
            for q in range(4):
                b.out_tiles[t, pl.ds(q * 8 + i, 8, 32), :] = value[q * 8 : q * 8 + 8]

        by_rows(8, body)
        return pltpu.make_async_copy(b.out_tiles.at[t], product.at[t], b.local_sem.at[4 + t])

    for copy in ends[:5]:
        copy.wait()
    stores = []
    for t in (1, 2, 0, 3):
        if t in (0, 3):
            ends[5 + t // 3].wait()
        stores.append(finish(t))
        stores[-1].start()
    for copy in halo + back + dual:
        pass
    for copy in stores:
        copy.wait()


def as_tiles(shard):
    split = shard.reshape(ROWS // 8, 8, CHUNKS, LANES)
    return split.transpose(0, 2, 1, 3).reshape(ROWS // 8, 8 * CHUNKS, LANES)


def solution(mesh):
    segments, slabs = mesh.shape["tm"], mesh.shape["space"]

    def shards(base_start, direction, damp_levels, damp_table):
        any_spec = pl.BlockSpec(memory_space=pl.ANY)
        result = pl.pallas_call(
            functools.partial(kernel, segments, slabs),
            out_shape=jax.ShapeDtypeStruct((ROWS // 8, 8 * CHUNKS, LANES), jnp.float32),
            in_specs=[any_spec] * 4,
            out_specs=any_spec,
            scratch_shapes=list(SCRATCH.values()),
            compiler_params=pltpu.CompilerParams(
                collective_id=0, has_side_effects=True, vmem_limit_bytes=60 * 2**20
            ),
        )(as_tiles(base_start), as_tiles(direction), damp_levels, damp_table)
        split = result.reshape(ROWS // 8, CHUNKS, 8, LANES).transpose(0, 2, 1, 3)
        return split.reshape(1, ROWS, COLS)

    in_specs = (P("tm", "space", None), P("tm", "space", None), P("space", None), P())
    out_specs = P("tm", "space", None)
    return jax.shard_map(shards, mesh=mesh, in_specs=in_specs, out_specs=out_specs, check_vma=False)
```

```python
import functools
import math

import jax
import jax.numpy as jnp
from jax import lax
from jax.experimental import pallas as pl
from jax.experimental.pallas import tpu as pltpu
from jax.sharding import PartitionSpec as P

MESH = pl.DeviceIdType.MESH

STEPS = 4
ROWS = 32
COLS = 4096
LANES = 128
CHUNKS = COLS // LANES
OFF = 16
HELD = ROWS + 2 * OFF

coef_lap = 0.05
coef_bih = 0.028
coef_slope = 0.05

_root = math.sqrt((coef_lap / coef_bih) ** 2 + 4.0 / coef_bih)
NEAR = 4.0 + (-coef_lap / coef_bih + _root) / 2.0
FAR = 4.0 + (-coef_lap / coef_bih - _root) / 2.0
SLOPE = coef_slope / (2.0 * coef_bih)
SCALE = coef_bih**STEPS


def beside(x):
    lane = lax.broadcasted_iota(jnp.int32, (1, 1, LANES), 2)
    turned = pltpu.roll(x[:, :8], LANES - 1, 2)
    last = jnp.where(lane == LANES - 1, pltpu.roll(turned, 7, 1), turned)
    turned = pltpu.roll(x[:, 24:], 1, 2)
    first = jnp.where(lane == 0, pltpu.roll(turned, 1, 1), turned)
    return jnp.concatenate([x[:, 8:], last], 1), jnp.concatenate([first, x[:, :24]], 1)


def permute(parts, order):
    x = jnp.concatenate(parts, 1)
    high = x.astype(jnp.bfloat16)
    rest = x - high.astype(jnp.float32)
    middle = rest.astype(jnp.bfloat16)
    low = (rest - middle.astype(jnp.float32)).astype(jnp.bfloat16)
    n = x.shape[0]
    out = jnp.dot(jnp.concatenate([high, middle, low], 0), order, preferred_element_type=jnp.float32)
    return (out[:n] + out[n : 2 * n]) + out[2 * n :]


def fill_orders(forth, back):
    for ref, source, target in ((forth, 0, 1), (back, 1, 0)):
        cell = lax.broadcasted_iota(jnp.int32, ref.shape, source)
        entry = lax.broadcasted_iota(jnp.int32, ref.shape, target)
        hit = cell == (entry % LANES) * 4 + entry // LANES
        ref[...] = jnp.where(hit, 1.0, 0.0).astype(jnp.bfloat16)


def over_rows(low, high, most, body):
    count = high - low + 1
    steps = -(-count // most)
    size = -(-count // steps)

    def step(i, carry):
        for j in range(size):
            body(low + OFF + i * size + j)
        return carry

    if steps == 1:
        step(0, 0)
    else:
        lax.fori_loop(0, steps, step, 0)


def cross_of(ref, r):
    return ref[pl.ds(r, 1)], ref[pl.ds(r - 1, 1)], ref[pl.ds(r + 1, 1)]


def forward_first(k, b, low, high, most, base=True, tangent=True):
    state, half, grad_x, grad_y = b.state.at[k], b.state_half.at[k], b.grad_x.at[k], b.grad_y.at[k]
    pert, pert_half, cross = b.pert.at[k], b.pert_half.at[k], b.cross.at[k]

    def body(r):
        row = pl.ds(r, 1)
        c, n, s = cross_of(state, r)
        right, left = beside(c)
        slope_x, slope_y = right - left, s - n
        grad_x[row] = slope_x
        grad_y[row] = slope_y
        if base:
            half[row] = ((right + left) + (n + s)) - NEAR * c
        if tangent:
            c, n, s = cross_of(pert, r)
            right, left = beside(c)
            pert_half[row] = ((right + left) + (n + s)) - NEAR * c
            cross[row] = slope_x * (right - left) + slope_y * (s - n)

    over_rows(low, high, most, body)


def forward_second(k, b, low, high, most, base=True, tangent=True):
    half, grad_x, grad_y = b.state_half.at[k], b.grad_x.at[k], b.grad_y.at[k]
    pert_half, cross, pert_next = b.pert_half.at[k], b.cross.at[k], b.pert.at[k + 1]
    if base:
        state_next = b.state.at[k + 1]

    def body(r):
        row = pl.ds(r, 1)
        if base:
            c, n, s = cross_of(half, r)
            right, left = beside(c)
            slope_x, slope_y = grad_x[row], grad_y[row]
            linear = ((right + left) + (n + s)) - FAR * c
            squares = slope_x * slope_x + slope_y * slope_y
            state_next[row] = linear * (-coef_bih) + squares * (-coef_bih / 2.0)
        if tangent:
            c, n, s = cross_of(pert_half, r)
            right, left = beside(c)
            pert_next[row] = (((right + left) + (n + s)) - FAR * c) + cross[row]

    over_rows(low, high, most, body)


def adjoint_first(k, b, low, high, most):
    dual, grad_x, grad_y = b.dual.at[k + 1], b.grad_x.at[k], b.grad_y.at[k]
    half, flux_dx, flux_y = b.dual_half.at[k], b.flux_dx.at[k], b.flux_y.at[k]

    def body(r):
        row = pl.ds(r, 1)
        c, n, s = cross_of(dual, r)
        right, left = beside(c)
        half[row] = ((right + left) + (n + s)) - NEAR * c
        right, left = beside(grad_x[row] * c)
        flux_dx[row] = right - left
        flux_y[row] = grad_y[row] * c

    over_rows(low, high, most, body)


def adjoint_second(k, b, low, high, most):
    half, flux_dx, flux_y, dual_next = b.dual_half.at[k], b.flux_dx.at[k], b.flux_y.at[k], b.dual.at[k]

    def body(r):
        c, n, s = cross_of(half, r)
        right, left = beside(c)
        spread = flux_dx[pl.ds(r, 1)] + (flux_y[pl.ds(r + 1, 1)] - flux_y[pl.ds(r - 1, 1)])
        dual_next[pl.ds(r, 1)] = (((right + left) + (n + s)) - FAR * c) - spread

    over_rows(low, high, most, body)


def by_rows(count, body):
    lax.fori_loop(0, count, lambda i, carry: (body(i), carry)[1], 0)


def interleave(tiles_in, order, dest, scale=None):
    parts = []
    for a in range(4):
        pieces = [tiles_in[t, pl.ds(a * 8 + i, 8, 32), :] for t in range(4) for i in range(8)]
        parts.append(jnp.concatenate(pieces, 0))
    out = permute(parts, order[...])
    for q in range(4):
        part = out[:, q * LANES : (q + 1) * LANES].reshape(ROWS, 8, LANES)
        dest[OFF : OFF + ROWS, q * 8 : q * 8 + 8, :] = part if scale is None else part * scale


class Buffers:
    def __init__(self, names, refs):
        self.__dict__.update(zip(names, refs, strict=True))


def row_buffer(*lead):
    return pltpu.VMEM((*lead, CHUNKS, LANES), jnp.float32)


def tiles(*lead):
    return pltpu.VMEM((*lead, 8 * CHUNKS, LANES), jnp.float32)


ENDS = ((14, 4), (10, 4), (18, 4), (8, 2), (22, 2), (0, 8), (24, 8))
BACK = ((0, 8), (24, 8), (8, 4), (20, 4), (12, 8))
HALO = (
    (True, 24, -8, True),
    (True, 0, 32, False),
    (False, 24, -8, True),
    (False, 0, 32, False),
    (False, 16, -16, True),
    (False, 8, 40, False),
)

SCRATCH = {
    "base_in": tiles(4),
    "dir_in": tiles(4),
    "out_tiles": tiles(4),
    "forth": pltpu.VMEM((4 * LANES, 4 * LANES), jnp.bfloat16),
    "back": pltpu.VMEM((4 * LANES, 4 * LANES), jnp.bfloat16),
    "next_rows": row_buffer(HELD),
    "prev_ends": row_buffer(HELD),
    "state": row_buffer(STEPS, HELD),
    "state_half": row_buffer(STEPS, HELD),
    "grad_x": row_buffer(STEPS, HELD),
    "grad_y": row_buffer(STEPS, HELD),
    "pert": row_buffer(STEPS + 1, HELD),
    "pert_half": row_buffer(STEPS, HELD),
    "cross": row_buffer(STEPS, HELD),
    "dual": row_buffer(STEPS + 1, HELD),
    "dual_half": row_buffer(STEPS, HELD),
    "flux_dx": row_buffer(STEPS, HELD),
    "flux_y": row_buffer(STEPS, HELD),
    "damp": pltpu.VMEM((4, 8, LANES), jnp.float32),
    "levels": pltpu.VMEM((4, CHUNKS), jnp.int32),
    "table": pltpu.SMEM((4,), jnp.float32),
    "local_sem": pltpu.SemaphoreType.DMA((12,)),
    "halo_send": pltpu.SemaphoreType.DMA((len(HALO),)),
    "halo_recv": pltpu.SemaphoreType.DMA((len(HALO),)),
    "back_send": pltpu.SemaphoreType.DMA((len(BACK),)),
    "back_recv": pltpu.SemaphoreType.DMA((len(BACK),)),
    "dual_send": pltpu.SemaphoreType.DMA((2,)),
    "dual_recv": pltpu.SemaphoreType.DMA((2,)),
    "ends_send": pltpu.SemaphoreType.DMA((len(ENDS),)),
    "ends_recv": pltpu.SemaphoreType.DMA((len(ENDS),)),
}


def kernel(segments, slabs, base, direction, levels, table, product, *scratch):
    b = Buffers(SCRATCH, scratch)
    tm, sp = lax.axis_index("tm"), lax.axis_index("space")
    after, before = lax.rem(tm + 1, segments), lax.rem(tm + segments - 1, segments)
    below, above = lax.rem(sp + 1, slabs), lax.rem(sp + slabs - 1, slabs)
    next_dev, prev_dev, down_dev, up_dev = (after, sp), (before, sp), (tm, below), (tm, above)

    barrier = pltpu.get_barrier_semaphore()
    for dev in (next_dev, prev_dev, down_dev, up_dev):
        pl.semaphore_signal(barrier, inc=1, device_id=dev, device_id_type=MESH)

    load = [
        pltpu.make_async_copy(base, b.base_in, b.local_sem.at[0]),
        pltpu.make_async_copy(direction, b.dir_in, b.local_sem.at[1]),
        pltpu.make_async_copy(levels, b.levels, b.local_sem.at[2]),
        pltpu.make_async_copy(table, b.table, b.local_sem.at[3]),
    ]
    for copy in load:
        copy.start()

    def remote(src, dst, send, recv, dev):
        return pltpu.make_async_remote_copy(
            src_ref=src, dst_ref=dst, send_sem=send, recv_sem=recv, device_id=dev, device_id_type=MESH
        )

    halo = []
    for i, (is_dir, src, dst, down) in enumerate(HALO):
        held = (b.pert if is_dir else b.state).at[0]
        halo.append(
            remote(
                held.at[pl.ds(OFF + src, 8)],
                held.at[pl.ds(OFF + dst, 8)],
                b.halo_send.at[i],
                b.halo_recv.at[i],
                down_dev if down else up_dev,
            )
        )
    back = []
    for i, (first, count) in enumerate(BACK):
        rows = pl.ds(OFF + first, count)
        back.append(remote(b.pert.at[0, rows], b.next_rows.at[rows], b.back_send.at[i], b.back_recv.at[i], prev_dev))
    ends = []
    for i, (first, count) in enumerate(ENDS):
        rows = pl.ds(OFF + first, count)
        ends.append(
            remote(b.pert.at[STEPS, rows], b.prev_ends.at[rows], b.ends_send.at[i], b.ends_recv.at[i], next_dev)
        )
    dual = [
        remote(
            b.dual.at[STEPS, pl.ds(OFF + src, 8)],
            b.dual.at[STEPS, pl.ds(OFF + dst, 8)],
            b.dual_send.at[i],
            b.dual_recv.at[i],
            dev,
        )
        for i, (src, dst, dev) in enumerate(((0, ROWS, up_dev), (ROWS - 8, -8, down_dev)))
    ]

    fill_orders(b.forth, b.back)
    load[1].wait()
    interleave(b.dir_in, b.forth, b.pert.at[0])
    pl.semaphore_wait(barrier, 4)
    for copy in back[:2] + halo[:2] + back[2:]:
        copy.start()
    load[0].wait()
    interleave(b.base_in, b.forth, b.state.at[0], SLOPE)
    for copy in halo[2:]:
        copy.start()

    def strip(k, low, high, sides, most):
        first_low = low - 1 if sides <= 0 else low + 1
        first_high = high + 1 if sides >= 0 else high - 1
        forward_first(k, b, first_low, first_high, most, base=k < STEPS - 1)
        forward_second(k, b, low, high, most, base=k < STEPS - 1)

    for k in range(STEPS):
        reach = 2 * (STEPS - 1 - k)
        strip(k, 14 - reach, 17 + reach, 0, 32)
    ends[0].start()
    for k in range(STEPS):
        reach = 2 * (STEPS - 1 - k)
        strip(k, 10 - reach, 13 - reach, -1, 32)
        strip(k, 18 + reach, 21 + reach, 1, 32)
    ends[1].start()
    ends[2].start()
    for k in range(STEPS):
        reach = 2 * (STEPS - 1 - k)
        strip(k, 8 - reach, 9 - reach, -1, 32)
        strip(k, 22 + reach, 23 + reach, 1, 32)
    ends[3].start()
    ends[4].start()

    for copy in halo[:4]:
        copy.wait()
    for k in range(STEPS):
        strip(k, -6 + 2 * k, 1 + 2 * k, -1, 8)
        strip(k, 30 - 2 * k, 37 - 2 * k, 1, 8)
    ends[5].start()
    ends[6].start()

    for copy in halo[4:]:
        copy.wait()
    for k in range(STEPS):
        last = k == STEPS - 1
        forward_first(k, b, -15 + 2 * k, -8 + 2 * k, 8, base=not last, tangent=False)
        forward_first(k, b, 39 - 2 * k, 46 - 2 * k, 8, base=not last, tangent=False)
        if not last:
            forward_second(k, b, -14 + 2 * k, -7 + 2 * k, 8, tangent=False)
            forward_second(k, b, 38 - 2 * k, 45 - 2 * k, 8, tangent=False)

    load[2].wait()
    load[3].wait()
    held = b.levels[...]
    coarse = jnp.zeros(held.shape, jnp.float32)
    for level in range(4):
        coarse = coarse + jnp.where(held == level, b.table[level], 0.0)
    entry = lax.broadcasted_iota(jnp.int32, (8, CHUNKS), 0)
    chunk = lax.broadcasted_iota(jnp.int32, (8, CHUNKS), 1)
    quarter = lax.broadcasted_iota(jnp.int32, (8, LANES), 1) // 32
    for t in range(4):
        value = jnp.zeros((8, LANES), jnp.float32)
        for a in range(4):
            own = jnp.where(chunk == 4 * entry + a, coarse[t : t + 1], 0.0)
            value = value + jnp.where(quarter == a, jnp.sum(own, axis=1, keepdims=True), 0.0)
        b.damp[t] = value

    def residual(first, count):
        rows = pl.ds(OFF + first, count)
        b.dual[STEPS, rows] = b.pert[STEPS, rows] * SCALE - b.next_rows[rows]

    for side in range(2):
        back[side].wait()
        residual(*BACK[side])
        dual[side].start()
    for i in (2, 3):
        back[i].wait()
        residual(*BACK[i])
    dual[0].wait()
    dual[1].wait()

    for k in range(STEPS - 1, -1, -1):
        far, near = -2 * k, 3 + 2 * k
        adjoint_first(k, b, far - 1, near + 1, 8)
        adjoint_first(k, b, 30 - near, 32 - far, 8)
        adjoint_second(k, b, far, near, 8)
        adjoint_second(k, b, 31 - near, 31 - far, 8)
    back[4].wait()
    residual(*BACK[4])
    for k in range(STEPS - 1, -1, -1):
        near = 3 + 2 * k
        adjoint_first(k, b, near + 2, 29 - near, 32)
        adjoint_second(k, b, near + 1, 30 - near, 32)

    def finish(tiles_done):
        parts = [[] for _ in range(4)]
        for t in tiles_done:
            scaled = 1.0 + jnp.concatenate([b.damp[t]] * 4, 0)
            for i in range(8):
                r = OFF + 8 * t + i
                value = (b.dual[0, r] - b.prev_ends[r]) * SCALE + scaled * b.pert[0, r]
                for q in range(4):
                    parts[q].append(value[8 * q : 8 * q + 8])
        out = permute([jnp.concatenate(part, 0) for part in parts], b.back[...])
        stores = []
        for j, t in enumerate(tiles_done):
            for i in range(8):
                for a in range(4):
                    value = out[64 * j + 8 * i : 64 * j + 8 * i + 8, a * LANES : (a + 1) * LANES]
                    b.out_tiles[t, pl.ds(a * 8 + i, 8, 32), :] = value
            stores.append(pltpu.make_async_copy(b.out_tiles.at[t], product.at[t], b.local_sem.at[4 + t]))
            stores[-1].start()
        return stores

    for copy in ends[:5]:
        copy.wait()
    stores = finish((1, 2))
    for copy in ends[5:]:
        copy.wait()
    stores += finish((0, 3))
    for copy in stores:
        copy.wait()


def as_tiles(shard):
    split = shard.reshape(ROWS // 8, 8, CHUNKS, LANES)
    return split.transpose(0, 2, 1, 3).reshape(ROWS // 8, 8 * CHUNKS, LANES)


def solution(mesh):
    segments, slabs = mesh.shape["tm"], mesh.shape["space"]

    def shards(base_start, direction, damp_levels, damp_table):
        any_spec = pl.BlockSpec(memory_space=pl.ANY)
        result = pl.pallas_call(
            functools.partial(kernel, segments, slabs),
            out_shape=jax.ShapeDtypeStruct((ROWS // 8, 8 * CHUNKS, LANES), jnp.float32),
            in_specs=[any_spec] * 4,
            out_specs=any_spec,
            scratch_shapes=list(SCRATCH.values()),
            compiler_params=pltpu.CompilerParams(
                collective_id=0, has_side_effects=True, vmem_limit_bytes=60 * 2**20
            ),
        )(as_tiles(base_start), as_tiles(direction), damp_levels, damp_table)
        split = result.reshape(ROWS // 8, CHUNKS, 8, LANES).transpose(0, 2, 1, 3)
        return split.reshape(1, ROWS, COLS)

    in_specs = (P("tm", "space", None), P("tm", "space", None), P("space", None), P())
    out_specs = P("tm", "space", None)
    return jax.shard_map(shards, mesh=mesh, in_specs=in_specs, out_specs=out_specs, check_vma=False)
```

```python
import functools
import math

import jax
import jax.numpy as jnp
from jax import lax
from jax.experimental import pallas as pl
from jax.experimental.pallas import tpu as pltpu
from jax.sharding import PartitionSpec as P

MESH = pl.DeviceIdType.MESH

STEPS = 4
ROWS = 32
COLS = 4096
LANES = 128
CHUNKS = COLS // LANES
OFF = 16
HELD = ROWS + 2 * OFF

coef_lap = 0.05
coef_bih = 0.028
coef_slope = 0.05

_root = math.sqrt((coef_lap / coef_bih) ** 2 + 4.0 / coef_bih)
NEAR = 4.0 + (-coef_lap / coef_bih + _root) / 2.0
FAR = 4.0 + (-coef_lap / coef_bih - _root) / 2.0
SLOPE = coef_slope / (2.0 * coef_bih)
SCALE = coef_bih**STEPS


def beside(x):
    lane = lax.broadcasted_iota(jnp.int32, (1, 1, LANES), 2)
    turned = pltpu.roll(x[:, :8], LANES - 1, 2)
    last = jnp.where(lane == LANES - 1, pltpu.roll(turned, 7, 1), turned)
    turned = pltpu.roll(x[:, 24:], 1, 2)
    first = jnp.where(lane == 0, pltpu.roll(turned, 1, 1), turned)
    return jnp.concatenate([x[:, 8:], last], 1), jnp.concatenate([first, x[:, :24]], 1)


def permute(parts, order):
    x = jnp.concatenate(parts, 1)
    high = x.astype(jnp.bfloat16)
    rest = x - high.astype(jnp.float32)
    middle = rest.astype(jnp.bfloat16)
    low = (rest - middle.astype(jnp.float32)).astype(jnp.bfloat16)
    n = x.shape[0]
    out = jnp.dot(jnp.concatenate([high, middle, low], 0), order, preferred_element_type=jnp.float32)
    return (out[:n] + out[n : 2 * n]) + out[2 * n :]


def order_of(shape, forth):
    cell = lax.broadcasted_iota(jnp.int32, shape, 0 if forth else 1)
    entry = lax.broadcasted_iota(jnp.int32, shape, 1 if forth else 0)
    return jnp.where(cell == (entry % LANES) * 4 + entry // LANES, 1.0, 0.0).astype(jnp.bfloat16)


def over_rows(low, high, most, body):
    count = high - low + 1
    steps = -(-count // most)
    size = -(-count // steps)

    def step(i, carry):
        for j in range(size):
            body(low + OFF + i * size + j)
        return carry

    if steps == 1:
        step(0, 0)
    else:
        lax.fori_loop(0, steps, step, 0)


def cross_of(ref, r):
    return ref[pl.ds(r, 1)], ref[pl.ds(r - 1, 1)], ref[pl.ds(r + 1, 1)]


def forward_first(k, b, low, high, most, base=True, tangent=True):
    state, half, grad_x, grad_y = b.state.at[k], b.state_half.at[k], b.grad_x.at[k], b.grad_y.at[k]
    pert, pert_half, cross = b.pert.at[k], b.pert_half.at[k], b.cross.at[k]

    def body(r):
        row = pl.ds(r, 1)
        c, n, s = cross_of(state, r)
        right, left = beside(c)
        slope_x, slope_y = right - left, s - n
        grad_x[row] = slope_x
        grad_y[row] = slope_y
        if base:
            half[row] = ((right + left) + (n + s)) - NEAR * c
        if tangent:
            c, n, s = cross_of(pert, r)
            right, left = beside(c)
            pert_half[row] = ((right + left) + (n + s)) - NEAR * c
            cross[row] = slope_x * (right - left) + slope_y * (s - n)

    over_rows(low, high, most, body)


def forward_second(k, b, low, high, most, base=True, tangent=True):
    half, grad_x, grad_y = b.state_half.at[k], b.grad_x.at[k], b.grad_y.at[k]
    pert_half, cross, pert_next = b.pert_half.at[k], b.cross.at[k], b.pert.at[k + 1]
    if base:
        state_next = b.state.at[k + 1]

    def body(r):
        row = pl.ds(r, 1)
        if base:
            c, n, s = cross_of(half, r)
            right, left = beside(c)
            slope_x, slope_y = grad_x[row], grad_y[row]
            linear = ((right + left) + (n + s)) - FAR * c
            squares = slope_x * slope_x + slope_y * slope_y
            state_next[row] = linear * (-coef_bih) + squares * (-coef_bih / 2.0)
        if tangent:
            c, n, s = cross_of(pert_half, r)
            right, left = beside(c)
            pert_next[row] = (((right + left) + (n + s)) - FAR * c) + cross[row]

    over_rows(low, high, most, body)


def adjoint_first(k, b, low, high, most):
    dual, grad_x, grad_y = b.dual.at[k + 1], b.grad_x.at[k], b.grad_y.at[k]
    half, flux_dx, flux_y = b.dual_half.at[k], b.flux_dx.at[k], b.flux_y.at[k]

    def body(r):
        row = pl.ds(r, 1)
        c, n, s = cross_of(dual, r)
        right, left = beside(c)
        half[row] = ((right + left) + (n + s)) - NEAR * c
        right, left = beside(grad_x[row] * c)
        flux_dx[row] = right - left
        flux_y[row] = grad_y[row] * c

    over_rows(low, high, most, body)


def adjoint_second(k, b, low, high, most):
    half, flux_dx, flux_y, dual_next = b.dual_half.at[k], b.flux_dx.at[k], b.flux_y.at[k], b.dual.at[k]

    def body(r):
        c, n, s = cross_of(half, r)
        right, left = beside(c)
        spread = flux_dx[pl.ds(r, 1)] + (flux_y[pl.ds(r + 1, 1)] - flux_y[pl.ds(r - 1, 1)])
        dual_next[pl.ds(r, 1)] = (((right + left) + (n + s)) - FAR * c) - spread

    over_rows(low, high, most, body)


def by_rows(count, body):
    lax.fori_loop(0, count, lambda i, carry: (body(i), carry)[1], 0)


def interleave(slabs_in, order, dests, scales):
    parts = []
    for a in range(4):
        pieces = [slab[t, pl.ds(a * 8 + i, 8, 32), :] for slab in slabs_in for t in range(4) for i in range(8)]
        parts.append(jnp.concatenate(pieces, 0))
    out = permute(parts, order[...])
    for j, (dest, scale) in enumerate(zip(dests, scales, strict=True)):
        for q in range(4):
            part = out[j * ROWS * 8 : (j + 1) * ROWS * 8, q * LANES : (q + 1) * LANES].reshape(ROWS, 8, LANES)
            dest[OFF : OFF + ROWS, q * 8 : q * 8 + 8, :] = part if scale is None else part * scale


class Buffers:
    def __init__(self, names, refs):
        self.__dict__.update(zip(names, refs, strict=True))


def row_buffer(*lead):
    return pltpu.VMEM((*lead, CHUNKS, LANES), jnp.float32)


def tiles(*lead):
    return pltpu.VMEM((*lead, 8 * CHUNKS, LANES), jnp.float32)


ENDS = ((14, 4), (10, 4), (18, 4), (8, 2), (22, 2), (0, 8), (24, 8))
BACK = ((0, 8), (24, 8), (8, 4), (20, 4), (12, 8))
HALO = (
    (True, 24, -8, True),
    (True, 0, 32, False),
    (False, 24, -8, True),
    (False, 0, 32, False),
    (False, 16, -16, True),
    (False, 8, 40, False),
)

SCRATCH = {
    "base_in": tiles(4),
    "dir_in": tiles(4),
    "forth": pltpu.VMEM((4 * LANES, 4 * LANES), jnp.bfloat16),
    "back": pltpu.VMEM((4 * LANES, 4 * LANES), jnp.bfloat16),
    "next_rows": row_buffer(HELD),
    "prev_ends": row_buffer(HELD),
    "state": row_buffer(STEPS, HELD),
    "state_half": row_buffer(STEPS, HELD),
    "grad_x": row_buffer(STEPS, HELD),
    "grad_y": row_buffer(STEPS, HELD),
    "pert": row_buffer(STEPS + 1, HELD),
    "pert_half": row_buffer(STEPS, HELD),
    "cross": row_buffer(STEPS, HELD),
    "dual": row_buffer(STEPS + 1, HELD),
    "dual_half": row_buffer(STEPS, HELD),
    "flux_dx": row_buffer(STEPS, HELD),
    "flux_y": row_buffer(STEPS, HELD),
    "damp": pltpu.VMEM((4, 8, LANES), jnp.float32),
    "levels": pltpu.VMEM((4, CHUNKS), jnp.int32),
    "table": pltpu.SMEM((4,), jnp.float32),
    "local_sem": pltpu.SemaphoreType.DMA((12,)),
    "halo_send": pltpu.SemaphoreType.DMA((len(HALO),)),
    "halo_recv": pltpu.SemaphoreType.DMA((len(HALO),)),
    "back_send": pltpu.SemaphoreType.DMA((len(BACK),)),
    "back_recv": pltpu.SemaphoreType.DMA((len(BACK),)),
    "dual_send": pltpu.SemaphoreType.DMA((2,)),
    "dual_recv": pltpu.SemaphoreType.DMA((2,)),
    "ends_send": pltpu.SemaphoreType.DMA((len(ENDS),)),
    "ends_recv": pltpu.SemaphoreType.DMA((len(ENDS),)),
}


def kernel(segments, slabs, base, direction, levels, table, product, *scratch):
    b = Buffers(SCRATCH, scratch)
    tm, sp = lax.axis_index("tm"), lax.axis_index("space")
    after, before = lax.rem(tm + 1, segments), lax.rem(tm + segments - 1, segments)
    below, above = lax.rem(sp + 1, slabs), lax.rem(sp + slabs - 1, slabs)
    next_dev, prev_dev, down_dev, up_dev = (after, sp), (before, sp), (tm, below), (tm, above)

    barrier = pltpu.get_barrier_semaphore()
    for dev in (next_dev, prev_dev, down_dev, up_dev):
        pl.semaphore_signal(barrier, inc=1, device_id=dev, device_id_type=MESH)

    load = [
        pltpu.make_async_copy(base, b.base_in, b.local_sem.at[0]),
        pltpu.make_async_copy(direction, b.dir_in, b.local_sem.at[1]),
        pltpu.make_async_copy(levels, b.levels, b.local_sem.at[2]),
        pltpu.make_async_copy(table, b.table, b.local_sem.at[3]),
    ]
    for copy in load:
        copy.start()

    def remote(src, dst, send, recv, dev):
        return pltpu.make_async_remote_copy(
            src_ref=src, dst_ref=dst, send_sem=send, recv_sem=recv, device_id=dev, device_id_type=MESH
        )

    halo = []
    for i, (is_dir, src, dst, down) in enumerate(HALO):
        held = (b.pert if is_dir else b.state).at[0]
        halo.append(
            remote(
                held.at[pl.ds(OFF + src, 8)],
                held.at[pl.ds(OFF + dst, 8)],
                b.halo_send.at[i],
                b.halo_recv.at[i],
                down_dev if down else up_dev,
            )
        )
    back = []
    for i, (first, count) in enumerate(BACK):
        rows = pl.ds(OFF + first, count)
        back.append(remote(b.pert.at[0, rows], b.next_rows.at[rows], b.back_send.at[i], b.back_recv.at[i], prev_dev))
    ends = []
    for i, (first, count) in enumerate(ENDS):
        rows = pl.ds(OFF + first, count)
        ends.append(
            remote(b.pert.at[STEPS, rows], b.prev_ends.at[rows], b.ends_send.at[i], b.ends_recv.at[i], next_dev)
        )
    dual = [
        remote(
            b.dual.at[STEPS, pl.ds(OFF + src, 8)],
            b.dual.at[STEPS, pl.ds(OFF + dst, 8)],
            b.dual_send.at[i],
            b.dual_recv.at[i],
            dev,
        )
        for i, (src, dst, dev) in enumerate(((0, ROWS, up_dev), (ROWS - 8, -8, down_dev)))
    ]

    b.forth[...] = order_of(b.forth.shape, True)
    load[1].wait()
    load[0].wait()
    interleave([b.dir_in, b.base_in], b.forth, [b.pert.at[0], b.state.at[0]], [None, SLOPE])
    pl.semaphore_wait(barrier, 4)
    for copy in halo[:2] + back[:1] + halo[2:4] + back[1:] + halo[4:]:
        copy.start()

    def strip(k, low, high, sides, most):
        first_low = low - 1 if sides <= 0 else low + 1
        first_high = high + 1 if sides >= 0 else high - 1
        forward_first(k, b, first_low, first_high, most, base=k < STEPS - 1)
        forward_second(k, b, low, high, most, base=k < STEPS - 1)

    for k in range(STEPS):
        reach = 2 * (STEPS - 1 - k)
        strip(k, 14 - reach, 17 + reach, 0, 32)
    ends[0].start()
    for k in range(STEPS):
        reach = 2 * (STEPS - 1 - k)
        strip(k, 10 - reach, 13 - reach, -1, 32)
        strip(k, 18 + reach, 21 + reach, 1, 32)
    ends[1].start()
    ends[2].start()
    for k in range(STEPS):
        reach = 2 * (STEPS - 1 - k)
        strip(k, 8 - reach, 9 - reach, -1, 32)
        strip(k, 22 + reach, 23 + reach, 1, 32)
    ends[3].start()
    ends[4].start()

    b.back[...] = order_of(b.back.shape, False)
    for copy in halo[:4]:
        copy.wait()
    for k in range(STEPS):
        strip(k, -6 + 2 * k, 1 + 2 * k, -1, 8)
        strip(k, 30 - 2 * k, 37 - 2 * k, 1, 8)
    ends[5].start()
    ends[6].start()

    def residual(first, count):
        rows = pl.ds(OFF + first, count)
        b.dual[STEPS, rows] = b.pert[STEPS, rows] * SCALE - b.next_rows[rows]

    for side in range(2):
        back[side].wait()
        residual(*BACK[side])
        dual[side].start()
    for copy in halo[4:]:
        copy.wait()
    for k in range(STEPS):
        last = k == STEPS - 1
        forward_first(k, b, -15 + 2 * k, -8 + 2 * k, 8, base=not last, tangent=False)
        forward_first(k, b, 39 - 2 * k, 46 - 2 * k, 8, base=not last, tangent=False)
        if not last:
            forward_second(k, b, -14 + 2 * k, -7 + 2 * k, 8, tangent=False)
            forward_second(k, b, 38 - 2 * k, 45 - 2 * k, 8, tangent=False)

    load[2].wait()
    load[3].wait()
    held = b.levels[...]
    coarse = jnp.zeros(held.shape, jnp.float32)
    for level in range(4):
        coarse = coarse + jnp.where(held == level, b.table[level], 0.0)
    entry = lax.broadcasted_iota(jnp.int32, (8, CHUNKS), 0)
    chunk = lax.broadcasted_iota(jnp.int32, (8, CHUNKS), 1)
    quarter = lax.broadcasted_iota(jnp.int32, (8, LANES), 1) // 32
    for t in range(4):
        value = jnp.zeros((8, LANES), jnp.float32)
        for a in range(4):
            own = jnp.where(chunk == 4 * entry + a, coarse[t : t + 1], 0.0)
            value = value + jnp.where(quarter == a, jnp.sum(own, axis=1, keepdims=True), 0.0)
        b.damp[t] = value

    for i in (2, 3):
        back[i].wait()
        residual(*BACK[i])
    dual[0].wait()
    dual[1].wait()

    for k in range(STEPS - 1, -1, -1):
        far, near = -2 * k, 3 + 2 * k
        adjoint_first(k, b, far - 1, near + 1, 8)
        adjoint_first(k, b, 30 - near, 32 - far, 8)
        adjoint_second(k, b, far, near, 8)
        adjoint_second(k, b, 31 - near, 31 - far, 8)
    back[4].wait()
    residual(*BACK[4])
    for k in range(STEPS - 1, -1, -1):
        near = 3 + 2 * k
        adjoint_first(k, b, near + 2, 29 - near, 32)
        adjoint_second(k, b, near + 1, 30 - near, 32)

    def finish(tiles_done):
        parts = [[] for _ in range(4)]
        for t in tiles_done:
            scaled = 1.0 + jnp.concatenate([b.damp[t]] * 4, 0)
            for i in range(8):
                r = OFF + 8 * t + i
                value = (b.dual[0, r] - b.prev_ends[r]) * SCALE + scaled * b.pert[0, r]
                for q in range(4):
                    parts[q].append(value[8 * q : 8 * q + 8])
        out = permute([jnp.concatenate(part, 0) for part in parts], b.back[...])
        for j, t in enumerate(tiles_done):
            for i in range(8):
                for a in range(4):
                    value = out[64 * j + 8 * i : 64 * j + 8 * i + 8, a * LANES : (a + 1) * LANES]
                    product[t, pl.ds(a * 8 + i, 8, 32), :] = value

    for copy in ends[:5]:
        copy.wait()
    finish((1, 2))
    for copy in ends[5:]:
        copy.wait()
    finish((0, 3))


def as_tiles(shard):
    split = shard.reshape(ROWS // 8, 8, CHUNKS, LANES)
    return split.transpose(0, 2, 1, 3).reshape(ROWS // 8, 8 * CHUNKS, LANES)


def solution(mesh):
    segments, slabs = mesh.shape["tm"], mesh.shape["space"]

    def shards(base_start, direction, damp_levels, damp_table):
        any_spec = pl.BlockSpec(memory_space=pl.ANY)
        result = pl.pallas_call(
            functools.partial(kernel, segments, slabs),
            out_shape=tiles(4),
            in_specs=[any_spec] * 4,
            out_specs=pl.BlockSpec(memory_space=pltpu.VMEM),
            scratch_shapes=list(SCRATCH.values()),
            compiler_params=pltpu.CompilerParams(
                collective_id=0, has_side_effects=True, vmem_limit_bytes=56 * 2**20
            ),
        )(as_tiles(base_start), as_tiles(direction), damp_levels, damp_table)
        split = result.reshape(ROWS // 8, CHUNKS, 8, LANES).transpose(0, 2, 1, 3)
        return split.reshape(1, ROWS, COLS)

    in_specs = (P("tm", "space", None), P("tm", "space", None), P("space", None), P())
    out_specs = P("tm", "space", None)
    return jax.shard_map(shards, mesh=mesh, in_specs=in_specs, out_specs=out_specs, check_vma=False)
```

```python
import functools
import math

import jax
import jax.numpy as jnp
from jax import lax
from jax.experimental import pallas as pl
from jax.experimental.pallas import tpu as pltpu
from jax.sharding import PartitionSpec as P

MESH = pl.DeviceIdType.MESH

STEPS = 4
ROWS = 32
COLS = 4096
LANES = 128
CHUNKS = COLS // LANES
OFF = 16
HELD = ROWS + 2 * OFF

coef_lap = 0.05
coef_bih = 0.028
coef_slope = 0.05

_root = math.sqrt((coef_lap / coef_bih) ** 2 + 4.0 / coef_bih)
NEAR = 4.0 + (-coef_lap / coef_bih + _root) / 2.0
FAR = 4.0 + (-coef_lap / coef_bih - _root) / 2.0
SLOPE = coef_slope / (2.0 * coef_bih)
SCALE = coef_bih**STEPS


def beside(x):
    lane = lax.broadcasted_iota(jnp.int32, (1, 1, LANES), 2)
    turned = pltpu.roll(x[:, :8], LANES - 1, 2)
    last = jnp.where(lane == LANES - 1, pltpu.roll(turned, 7, 1), turned)
    turned = pltpu.roll(x[:, 24:], 1, 2)
    first = jnp.where(lane == 0, pltpu.roll(turned, 1, 1), turned)
    return jnp.concatenate([x[:, 8:], last], 1), jnp.concatenate([first, x[:, :24]], 1)


def permute(parts, order):
    x = jnp.concatenate(parts, 1)
    high = x.astype(jnp.bfloat16)
    rest = x - high.astype(jnp.float32)
    middle = rest.astype(jnp.bfloat16)
    low = (rest - middle.astype(jnp.float32)).astype(jnp.bfloat16)
    n = x.shape[0]
    out = jnp.dot(jnp.concatenate([high, middle, low], 0), order, preferred_element_type=jnp.float32)
    return (out[:n] + out[n : 2 * n]) + out[2 * n :]


def order_of(shape, forth):
    cell = lax.broadcasted_iota(jnp.int32, shape, 0 if forth else 1)
    entry = lax.broadcasted_iota(jnp.int32, shape, 1 if forth else 0)
    return jnp.where(cell == (entry % LANES) * 4 + entry // LANES, 1.0, 0.0).astype(jnp.bfloat16)


def over_rows(low, count, most, body):
    steps = -(-count // most)
    size = -(-count // steps)

    def step(i, carry):
        for j in range(size):
            body(low + OFF + i * size + j)
        return carry

    if steps == 1:
        step(0, 0)
    else:
        lax.fori_loop(0, steps, step, 0)


def cross_of(ref, r):
    return ref[pl.ds(r, 1)], ref[pl.ds(r - 1, 1)], ref[pl.ds(r + 1, 1)]


def forward_first(k, b, low, count, most, base=True, tangent=True):
    state, half, grad_x, grad_y = b.state.at[k], b.state_half.at[k], b.grad_x.at[k], b.grad_y.at[k]
    pert, pert_half, cross = b.pert.at[k], b.pert_half.at[k], b.cross.at[k]

    def body(r):
        row = pl.ds(r, 1)
        c, n, s = cross_of(state, r)
        right, left = beside(c)
        slope_x, slope_y = right - left, s - n
        grad_x[row] = slope_x
        grad_y[row] = slope_y
        if base:
            half[row] = ((right + left) + (n + s)) - NEAR * c
        if tangent:
            c, n, s = cross_of(pert, r)
            right, left = beside(c)
            pert_half[row] = ((right + left) + (n + s)) - NEAR * c
            cross[row] = slope_x * (right - left) + slope_y * (s - n)

    over_rows(low, count, most, body)


def forward_second(k, b, low, count, most, base=True, tangent=True):
    half, grad_x, grad_y = b.state_half.at[k], b.grad_x.at[k], b.grad_y.at[k]
    pert_half, cross, pert_next = b.pert_half.at[k], b.cross.at[k], b.pert.at[k + 1]
    if base:
        state_next = b.state.at[k + 1]

    def body(r):
        row = pl.ds(r, 1)
        if base:
            c, n, s = cross_of(half, r)
            right, left = beside(c)
            slope_x, slope_y = grad_x[row], grad_y[row]
            linear = ((right + left) + (n + s)) - FAR * c
            squares = slope_x * slope_x + slope_y * slope_y
            state_next[row] = linear * (-coef_bih) + squares * (-coef_bih / 2.0)
        if tangent:
            c, n, s = cross_of(pert_half, r)
            right, left = beside(c)
            pert_next[row] = (((right + left) + (n + s)) - FAR * c) + cross[row]

    over_rows(low, count, most, body)


def adjoint_first(k, b, low, count, most):
    dual, grad_x, grad_y = b.dual.at[k + 1], b.grad_x.at[k], b.grad_y.at[k]
    half, flux_dx, flux_y = b.dual_half.at[k], b.flux_dx.at[k], b.flux_y.at[k]

    def body(r):
        row = pl.ds(r, 1)
        c, n, s = cross_of(dual, r)
        right, left = beside(c)
        half[row] = ((right + left) + (n + s)) - NEAR * c
        right, left = beside(grad_x[row] * c)
        flux_dx[row] = right - left
        flux_y[row] = grad_y[row] * c

    over_rows(low, count, most, body)


def adjoint_second(k, b, low, count, most):
    half, flux_dx, flux_y, dual_next = b.dual_half.at[k], b.flux_dx.at[k], b.flux_y.at[k], b.dual.at[k]

    def body(r):
        c, n, s = cross_of(half, r)
        right, left = beside(c)
        spread = flux_dx[pl.ds(r, 1)] + (flux_y[pl.ds(r + 1, 1)] - flux_y[pl.ds(r - 1, 1)])
        dual_next[pl.ds(r, 1)] = (((right + left) + (n + s)) - FAR * c) - spread

    over_rows(low, count, most, body)


def by_rows(count, body):
    lax.fori_loop(0, count, lambda i, carry: (body(i), carry)[1], 0)


def interleave(slabs_in, order, dests, scales):
    parts = []
    for a in range(4):
        pieces = [slab[t, pl.ds(a * 8 + i, 8, 32), :] for slab in slabs_in for t in range(4) for i in range(8)]
        parts.append(jnp.concatenate(pieces, 0))
    out = permute(parts, order[...])
    for j, (dest, scale) in enumerate(zip(dests, scales, strict=True)):
        for q in range(4):
            part = out[j * ROWS * 8 : (j + 1) * ROWS * 8, q * LANES : (q + 1) * LANES].reshape(ROWS, 8, LANES)
            dest[OFF : OFF + ROWS, q * 8 : q * 8 + 8, :] = part if scale is None else part * scale


class Buffers:
    def __init__(self, names, refs):
        self.__dict__.update(zip(names, refs, strict=True))


def row_buffer(*lead):
    return pltpu.VMEM((*lead, CHUNKS, LANES), jnp.float32)


def tiles(*lead):
    return pltpu.VMEM((*lead, 8 * CHUNKS, LANES), jnp.float32)


ENDS = ((14, 4), (10, 4), (18, 4), (8, 2), (22, 2), (0, 8), (24, 8))
BACK = ((0, 8), (24, 8), (8, 4), (20, 4), (12, 8))
HALO = (
    (True, 24, -8, True),
    (True, 0, 32, False),
    (False, 24, -8, True),
    (False, 0, 32, False),
    (False, 16, -16, True),
    (False, 8, 40, False),
)

SCRATCH = {
    "base_in": tiles(4),
    "dir_in": tiles(4),
    "forth": pltpu.VMEM((4 * LANES, 4 * LANES), jnp.bfloat16),
    "back": pltpu.VMEM((4 * LANES, 4 * LANES), jnp.bfloat16),
    "next_rows": row_buffer(HELD),
    "prev_ends": row_buffer(HELD),
    "state": row_buffer(STEPS, HELD),
    "state_half": row_buffer(STEPS, HELD),
    "grad_x": row_buffer(STEPS, HELD),
    "grad_y": row_buffer(STEPS, HELD),
    "pert": row_buffer(STEPS + 1, HELD),
    "pert_half": row_buffer(STEPS, HELD),
    "cross": row_buffer(STEPS, HELD),
    "dual": row_buffer(STEPS + 1, HELD),
    "dual_half": row_buffer(STEPS, HELD),
    "flux_dx": row_buffer(STEPS, HELD),
    "flux_y": row_buffer(STEPS, HELD),
    "damp": pltpu.VMEM((4, 8, LANES), jnp.float32),
    "levels": pltpu.VMEM((4, CHUNKS), jnp.int32),
    "table": pltpu.SMEM((4,), jnp.float32),
    "local_sem": pltpu.SemaphoreType.DMA((12,)),
    "halo_send": pltpu.SemaphoreType.DMA((len(HALO),)),
    "halo_recv": pltpu.SemaphoreType.DMA((len(HALO),)),
    "back_send": pltpu.SemaphoreType.DMA((len(BACK),)),
    "back_recv": pltpu.SemaphoreType.DMA((len(BACK),)),
    "dual_send": pltpu.SemaphoreType.DMA((2,)),
    "dual_recv": pltpu.SemaphoreType.DMA((2,)),
    "ends_send": pltpu.SemaphoreType.DMA((len(ENDS),)),
    "ends_recv": pltpu.SemaphoreType.DMA((len(ENDS),)),
}


def kernel(segments, slabs, base, direction, levels, table, product, *scratch):
    b = Buffers(SCRATCH, scratch)
    tm, sp = lax.axis_index("tm"), lax.axis_index("space")
    after, before = lax.rem(tm + 1, segments), lax.rem(tm + segments - 1, segments)
    below, above = lax.rem(sp + 1, slabs), lax.rem(sp + slabs - 1, slabs)
    next_dev, prev_dev, down_dev, up_dev = (after, sp), (before, sp), (tm, below), (tm, above)
    even = lax.rem(sp, 2) == 0
    lower_first = even | (sp == slabs - 1)

    def back_row(i):
        first, count = BACK[i]
        return first if i == 4 else jnp.where(even, first, ROWS - count - first)


    barrier = pltpu.get_barrier_semaphore()
    for dev in (next_dev, prev_dev, down_dev, up_dev):
        pl.semaphore_signal(barrier, inc=1, device_id=dev, device_id_type=MESH)

    load = [
        pltpu.make_async_copy(base, b.base_in, b.local_sem.at[0]),
        pltpu.make_async_copy(direction, b.dir_in, b.local_sem.at[1]),
        pltpu.make_async_copy(levels, b.levels, b.local_sem.at[2]),
        pltpu.make_async_copy(table, b.table, b.local_sem.at[3]),
    ]
    for copy in load:
        copy.start()

    def remote(src, dst, send, recv, dev):
        return pltpu.make_async_remote_copy(
            src_ref=src, dst_ref=dst, send_sem=send, recv_sem=recv, device_id=dev, device_id_type=MESH
        )

    halo = []
    for i, (is_dir, src, dst, down) in enumerate(HALO):
        held = (b.pert if is_dir else b.state).at[0]
        halo.append(
            remote(
                held.at[pl.ds(OFF + src, 8)],
                held.at[pl.ds(OFF + dst, 8)],
                b.halo_send.at[i],
                b.halo_recv.at[i],
                down_dev if down else up_dev,
            )
        )
    back = []
    for i, (_, count) in enumerate(BACK):
        rows = pl.ds(OFF + back_row(i), count)
        back.append(remote(b.pert.at[0, rows], b.next_rows.at[rows], b.back_send.at[i], b.back_recv.at[i], prev_dev))
    ends = []
    for i, (first, count) in enumerate(ENDS):
        rows = pl.ds(OFF + first, count)
        ends.append(
            remote(b.pert.at[STEPS, rows], b.prev_ends.at[rows], b.ends_send.at[i], b.ends_recv.at[i], next_dev)
        )
    dual = []
    for i in range(2):
        down = ~even if i == 0 else even
        src, dst = jnp.where(down, ROWS - 8, 0), jnp.where(down, -8, ROWS)
        sem = jnp.where(down, 0, 1)
        dual.append(
            remote(
                b.dual.at[STEPS, pl.ds(OFF + src, 8)],
                b.dual.at[STEPS, pl.ds(OFF + dst, 8)],
                b.dual_send.at[sem],
                b.dual_recv.at[sem],
                (tm, jnp.where(down, below, above)),
            )
        )

    def dual_arrived(lower):
        rows = b.dual.at[STEPS, pl.ds(OFF + jnp.where(lower, ROWS, -8), 8)]
        sem = jnp.where(lower, 1, 0)
        remote(rows, rows, b.dual_send.at[sem], b.dual_recv.at[sem], up_dev).wait_recv()

    b.forth[...] = order_of(b.forth.shape, True)
    load[1].wait()
    load[0].wait()
    interleave([b.dir_in, b.base_in], b.forth, [b.pert.at[0], b.state.at[0]], [None, SLOPE])
    pl.semaphore_wait(barrier, 4)
    for copy in halo[:2] + back[:1] + halo[2:4] + back[1:] + halo[4:]:
        copy.start()

    def strip(k, low, high, sides, most):
        first_low = low - 1 if sides <= 0 else low + 1
        first_high = high + 1 if sides >= 0 else high - 1
        forward_first(k, b, first_low, first_high - first_low + 1, most, base=k < STEPS - 1)
        forward_second(k, b, low, high - low + 1, most, base=k < STEPS - 1)

    for k in range(STEPS):
        reach = 2 * (STEPS - 1 - k)
        strip(k, 14 - reach, 17 + reach, 0, 32)
    ends[0].start()
    for k in range(STEPS):
        reach = 2 * (STEPS - 1 - k)
        strip(k, 10 - reach, 13 - reach, -1, 32)
        strip(k, 18 + reach, 21 + reach, 1, 32)
    ends[1].start()
    ends[2].start()
    for k in range(STEPS):
        reach = 2 * (STEPS - 1 - k)
        strip(k, 8 - reach, 9 - reach, -1, 32)
        strip(k, 22 + reach, 23 + reach, 1, 32)
    ends[3].start()
    ends[4].start()

    b.back[...] = order_of(b.back.shape, False)
    for copy in halo[:4]:
        copy.wait()
    for k in range(STEPS):
        strip(k, -6 + 2 * k, 1 + 2 * k, -1, 8)
        strip(k, 30 - 2 * k, 37 - 2 * k, 1, 8)
    ends[5].start()
    ends[6].start()

    def residual(first, count):
        rows = pl.ds(OFF + first, count)
        b.dual[STEPS, rows] = b.pert[STEPS, rows] * SCALE - b.next_rows[rows]

    for side in range(2):
        back[side].wait()
        residual(back_row(side), 8)
        dual[side].start()
    for copy in halo[4:]:
        copy.wait()
    for k in range(STEPS):
        last = k == STEPS - 1
        forward_first(k, b, -15 + 2 * k, 8, 8, base=not last, tangent=False)
        forward_first(k, b, 39 - 2 * k, 8, 8, base=not last, tangent=False)
        if not last:
            forward_second(k, b, -14 + 2 * k, 8, 8, tangent=False)
            forward_second(k, b, 38 - 2 * k, 8, 8, tangent=False)

    load[2].wait()
    load[3].wait()
    held = b.levels[...]
    coarse = jnp.zeros(held.shape, jnp.float32)
    for level in range(4):
        coarse = coarse + jnp.where(held == level, b.table[level], 0.0)
    entry = lax.broadcasted_iota(jnp.int32, (8, CHUNKS), 0)
    chunk = lax.broadcasted_iota(jnp.int32, (8, CHUNKS), 1)
    quarter = lax.broadcasted_iota(jnp.int32, (8, LANES), 1) // 32
    for t in range(4):
        value = jnp.zeros((8, LANES), jnp.float32)
        for a in range(4):
            own = jnp.where(chunk == 4 * entry + a, coarse[t : t + 1], 0.0)
            value = value + jnp.where(quarter == a, jnp.sum(own, axis=1, keepdims=True), 0.0)
        b.damp[t] = value

    def turned(first, count):
        return jnp.where(lower_first, first, ROWS - count - first)

    for i in (2, 3):
        back[i].wait()
        residual(back_row(i), 4)
    dual_arrived(lower_first)
    for k in range(STEPS - 1, -1, -1):
        adjoint_first(k, b, turned(27 - 2 * k, 6 + 4 * k), 6 + 4 * k, 32)
        adjoint_second(k, b, turned(28 - 2 * k, 4 + 4 * k), 4 + 4 * k, 32)
    back[4].wait()
    residual(*BACK[4])
    for k in range(STEPS - 1, -1, -1):
        adjoint_first(k, b, turned(7 - 2 * k, 20), 20, 32)
        adjoint_second(k, b, turned(8 - 2 * k, 20), 20, 32)

    def finish(tiles_done):
        parts = [[] for _ in range(4)]
        for t in tiles_done:
            scaled = 1.0 + jnp.concatenate([b.damp[t]] * 4, 0)
            for i in range(8):
                r = OFF + 8 * t + i
                value = (b.dual[0, r] - b.prev_ends[r]) * SCALE + scaled * b.pert[0, r]
                for q in range(4):
                    parts[q].append(value[8 * q : 8 * q + 8])
        out = permute([jnp.concatenate(part, 0) for part in parts], b.back[...])
        for j, t in enumerate(tiles_done):
            for i in range(8):
                for a in range(4):
                    value = out[64 * j + 8 * i : 64 * j + 8 * i + 8, a * LANES : (a + 1) * LANES]
                    product[t, pl.ds(a * 8 + i, 8, 32), :] = value

    dual_arrived(~lower_first)
    for copy in dual:
        copy.wait_send()
    for k in range(STEPS - 1, -1, -1):
        adjoint_first(k, b, turned(-2 * k - 1, 8), 8, 8)
        adjoint_second(k, b, turned(-2 * k, 8), 8, 8)
    for copy in ends[:5]:
        copy.wait()
    finish((1, 2))
    for copy in ends[5:]:
        copy.wait()
    finish((0, 3))


def as_tiles(shard):
    split = shard.reshape(ROWS // 8, 8, CHUNKS, LANES)
    return split.transpose(0, 2, 1, 3).reshape(ROWS // 8, 8 * CHUNKS, LANES)


def solution(mesh):
    segments, slabs = mesh.shape["tm"], mesh.shape["space"]

    def shards(base_start, direction, damp_levels, damp_table):
        any_spec = pl.BlockSpec(memory_space=pl.ANY)
        result = pl.pallas_call(
            functools.partial(kernel, segments, slabs),
            out_shape=tiles(4),
            in_specs=[any_spec] * 4,
            out_specs=pl.BlockSpec(memory_space=pltpu.VMEM),
            scratch_shapes=list(SCRATCH.values()),
            compiler_params=pltpu.CompilerParams(
                collective_id=0, has_side_effects=True, vmem_limit_bytes=56 * 2**20
            ),
        )(as_tiles(base_start), as_tiles(direction), damp_levels, damp_table)
        split = result.reshape(ROWS // 8, CHUNKS, 8, LANES).transpose(0, 2, 1, 3)
        return split.reshape(1, ROWS, COLS)

    in_specs = (P("tm", "space", None), P("tm", "space", None), P("space", None), P())
    out_specs = P("tm", "space", None)
    return jax.shard_map(shards, mesh=mesh, in_specs=in_specs, out_specs=out_specs, check_vma=False)
```

```python
import functools
import math

import jax
import jax.numpy as jnp
from jax import lax
from jax.experimental import pallas as pl
from jax.experimental.pallas import tpu as pltpu
from jax.sharding import PartitionSpec as P

MESH = pl.DeviceIdType.MESH

STEPS = 4
ROWS = 32
COLS = 4096
LANES = 128
CHUNKS = COLS // LANES
OFF = 16
HELD = ROWS + 2 * OFF

coef_lap = 0.05
coef_bih = 0.028
coef_slope = 0.05

_root = math.sqrt((coef_lap / coef_bih) ** 2 + 4.0 / coef_bih)
NEAR = 4.0 + (-coef_lap / coef_bih + _root) / 2.0
FAR = 4.0 + (-coef_lap / coef_bih - _root) / 2.0
SLOPE = coef_slope / (2.0 * coef_bih)
SCALE = coef_bih**STEPS


def beside(x):
    lane = lax.broadcasted_iota(jnp.int32, (1, 1, LANES), 2)
    turned = pltpu.roll(x[:, :8], LANES - 1, 2)
    last = jnp.where(lane == LANES - 1, pltpu.roll(turned, 7, 1), turned)
    turned = pltpu.roll(x[:, 24:], 1, 2)
    first = jnp.where(lane == 0, pltpu.roll(turned, 1, 1), turned)
    return jnp.concatenate([x[:, 8:], last], 1), jnp.concatenate([first, x[:, :24]], 1)


def permute(parts, order):
    x = jnp.concatenate(parts, 1)
    high = x.astype(jnp.bfloat16)
    rest = x - high.astype(jnp.float32)
    middle = rest.astype(jnp.bfloat16)
    low = (rest - middle.astype(jnp.float32)).astype(jnp.bfloat16)
    n = x.shape[0]
    out = jnp.dot(jnp.concatenate([high, middle, low], 0), order, preferred_element_type=jnp.float32)
    return (out[:n] + out[n : 2 * n]) + out[2 * n :]


def order_of(shape, forth):
    cell = lax.broadcasted_iota(jnp.int32, shape, 0 if forth else 1)
    entry = lax.broadcasted_iota(jnp.int32, shape, 1 if forth else 0)
    return jnp.where(cell == (entry % LANES) * 4 + entry // LANES, 1.0, 0.0).astype(jnp.bfloat16)


def over_rows(low, count, most, body):
    steps = -(-count // most)
    size = -(-count // steps)

    def step(i, carry):
        for j in range(size):
            body(low + OFF + i * size + j)
        return carry

    if steps == 1:
        step(0, 0)
    else:
        lax.fori_loop(0, steps, step, 0)


def cross_of(ref, r):
    return ref[pl.ds(r, 1)], ref[pl.ds(r - 1, 1)], ref[pl.ds(r + 1, 1)]


def forward_first(k, b, low, count, most, base=True, tangent=True):
    state, half, grad_x, grad_y = b.state.at[k], b.state_half.at[k], b.grad_x.at[k], b.grad_y.at[k]
    pert, pert_half, cross = b.pert.at[k], b.pert_half.at[k], b.cross.at[k]

    def body(r):
        row = pl.ds(r, 1)
        c, n, s = cross_of(state, r)
        right, left = beside(c)
        slope_x, slope_y = right - left, s - n
        grad_x[row] = slope_x
        grad_y[row] = slope_y
        if base:
            half[row] = ((right + left) + (n + s)) - NEAR * c
        if tangent:
            c, n, s = cross_of(pert, r)
            right, left = beside(c)
            pert_half[row] = ((right + left) + (n + s)) - NEAR * c
            cross[row] = slope_x * (right - left) + slope_y * (s - n)

    over_rows(low, count, most, body)


def forward_second(k, b, low, count, most, base=True, tangent=True):
    half, grad_x, grad_y = b.state_half.at[k], b.grad_x.at[k], b.grad_y.at[k]
    pert_half, cross, pert_next = b.pert_half.at[k], b.cross.at[k], b.pert.at[k + 1]
    if base:
        state_next = b.state.at[k + 1]

    def body(r):
        row = pl.ds(r, 1)
        if base:
            c, n, s = cross_of(half, r)
            right, left = beside(c)
            slope_x, slope_y = grad_x[row], grad_y[row]
            linear = ((right + left) + (n + s)) - FAR * c
            squares = slope_x * slope_x + slope_y * slope_y
            state_next[row] = linear * (-coef_bih) + squares * (-coef_bih / 2.0)
        if tangent:
            c, n, s = cross_of(pert_half, r)
            right, left = beside(c)
            pert_next[row] = (((right + left) + (n + s)) - FAR * c) + cross[row]

    over_rows(low, count, most, body)


def adjoint_first(k, b, low, count, most):
    dual, grad_x, grad_y = b.dual.at[k + 1], b.grad_x.at[k], b.grad_y.at[k]
    half, flux_dx, flux_y = b.dual_half.at[k], b.flux_dx.at[k], b.flux_y.at[k]

    def body(r):
        row = pl.ds(r, 1)
        c, n, s = cross_of(dual, r)
        right, left = beside(c)
        half[row] = ((right + left) + (n + s)) - NEAR * c
        right, left = beside(grad_x[row] * c)
        flux_dx[row] = right - left
        flux_y[row] = grad_y[row] * c

    over_rows(low, count, most, body)


def adjoint_second(k, b, low, count, most):
    half, flux_dx, flux_y, dual_next = b.dual_half.at[k], b.flux_dx.at[k], b.flux_y.at[k], b.dual.at[k]

    def body(r):
        c, n, s = cross_of(half, r)
        right, left = beside(c)
        spread = flux_dx[pl.ds(r, 1)] + (flux_y[pl.ds(r + 1, 1)] - flux_y[pl.ds(r - 1, 1)])
        dual_next[pl.ds(r, 1)] = (((right + left) + (n + s)) - FAR * c) - spread

    over_rows(low, count, most, body)


def by_rows(count, body):
    lax.fori_loop(0, count, lambda i, carry: (body(i), carry)[1], 0)


def interleave(slabs_in, order, dests, scales):
    parts = []
    for a in range(4):
        pieces = [slab[t, pl.ds(a * 8 + i, 8, 32), :] for slab in slabs_in for t in range(4) for i in range(8)]
        parts.append(jnp.concatenate(pieces, 0))
    out = permute(parts, order[...])
    for j, (dest, scale) in enumerate(zip(dests, scales, strict=True)):
        for q in range(4):
            part = out[j * ROWS * 8 : (j + 1) * ROWS * 8, q * LANES : (q + 1) * LANES].reshape(ROWS, 8, LANES)
            dest[OFF : OFF + ROWS, q * 8 : q * 8 + 8, :] = part if scale is None else part * scale


class Buffers:
    def __init__(self, names, refs):
        self.__dict__.update(zip(names, refs, strict=True))


def row_buffer(*lead):
    return pltpu.VMEM((*lead, CHUNKS, LANES), jnp.float32)


def tiles(*lead):
    return pltpu.VMEM((*lead, 8 * CHUNKS, LANES), jnp.float32)


ENDS = ((14, 4), (10, 4), (18, 4), (8, 2), (22, 2), (0, 8), (24, 8))
BACK = ((0, 8), (24, 8), (8, 4), (20, 4), (12, 8))
HALO = (
    (True, 24, -8, True),
    (True, 0, 32, False),
    (False, 24, -8, True),
    (False, 0, 32, False),
    (False, 16, -16, True),
    (False, 8, 40, False),
)

SCRATCH = {
    "base_in": tiles(4),
    "dir_in": tiles(4),
    "forth": pltpu.VMEM((4 * LANES, 4 * LANES), jnp.bfloat16),
    "back": pltpu.VMEM((4 * LANES, 4 * LANES), jnp.bfloat16),
    "next_rows": row_buffer(HELD),
    "prev_ends": row_buffer(HELD),
    "state": row_buffer(STEPS, HELD),
    "state_half": row_buffer(STEPS, HELD),
    "grad_x": row_buffer(STEPS, HELD),
    "grad_y": row_buffer(STEPS, HELD),
    "pert": row_buffer(STEPS + 1, HELD),
    "pert_half": row_buffer(STEPS, HELD),
    "cross": row_buffer(STEPS, HELD),
    "dual": row_buffer(STEPS + 1, HELD),
    "dual_half": row_buffer(STEPS, HELD),
    "flux_dx": row_buffer(STEPS, HELD),
    "flux_y": row_buffer(STEPS, HELD),
    "damp": pltpu.VMEM((4, 8, LANES), jnp.float32),
    "levels": pltpu.VMEM((4, CHUNKS), jnp.int32),
    "table": pltpu.SMEM((4,), jnp.float32),
    "local_sem": pltpu.SemaphoreType.DMA((12,)),
    "halo_send": pltpu.SemaphoreType.DMA((len(HALO),)),
    "halo_recv": pltpu.SemaphoreType.DMA((len(HALO),)),
    "back_send": pltpu.SemaphoreType.DMA((len(BACK),)),
    "back_recv": pltpu.SemaphoreType.DMA((len(BACK),)),
    "dual_send": pltpu.SemaphoreType.DMA((2,)),
    "dual_recv": pltpu.SemaphoreType.DMA((2,)),
    "ends_send": pltpu.SemaphoreType.DMA((len(ENDS),)),
    "ends_recv": pltpu.SemaphoreType.DMA((len(ENDS),)),
}


def kernel(segments, slabs, base, direction, levels, table, product, *scratch):
    b = Buffers(SCRATCH, scratch)
    tm, sp = lax.axis_index("tm"), lax.axis_index("space")
    after, before = lax.rem(tm + 1, segments), lax.rem(tm + segments - 1, segments)
    below, above = lax.rem(sp + 1, slabs), lax.rem(sp + slabs - 1, slabs)
    next_dev, prev_dev, down_dev, up_dev = (after, sp), (before, sp), (tm, below), (tm, above)
    even = lax.rem(sp, 2) == 0
    lower_first = (even & (sp != slabs // 2)) | (sp == slabs - 1) | (sp == 1)

    def back_row(i):
        first, count = BACK[i]
        return first if i == 4 else jnp.where(even, first, ROWS - count - first)


    barrier = pltpu.get_barrier_semaphore()
    for dev in (next_dev, prev_dev, down_dev, up_dev):
        pl.semaphore_signal(barrier, inc=1, device_id=dev, device_id_type=MESH)

    load = [
        pltpu.make_async_copy(base, b.base_in, b.local_sem.at[0]),
        pltpu.make_async_copy(direction, b.dir_in, b.local_sem.at[1]),
        pltpu.make_async_copy(levels, b.levels, b.local_sem.at[2]),
        pltpu.make_async_copy(table, b.table, b.local_sem.at[3]),
    ]
    for copy in load:
        copy.start()

    def remote(src, dst, send, recv, dev):
        return pltpu.make_async_remote_copy(
            src_ref=src, dst_ref=dst, send_sem=send, recv_sem=recv, device_id=dev, device_id_type=MESH
        )

    halo = []
    for i, (is_dir, src, dst, down) in enumerate(HALO):
        held = (b.pert if is_dir else b.state).at[0]
        halo.append(
            remote(
                held.at[pl.ds(OFF + src, 8)],
                held.at[pl.ds(OFF + dst, 8)],
                b.halo_send.at[i],
                b.halo_recv.at[i],
                down_dev if down else up_dev,
            )
        )
    back = []
    for i, (_, count) in enumerate(BACK):
        rows = pl.ds(OFF + back_row(i), count)
        back.append(remote(b.pert.at[0, rows], b.next_rows.at[rows], b.back_send.at[i], b.back_recv.at[i], prev_dev))
    ends = []
    for i, (first, count) in enumerate(ENDS):
        rows = pl.ds(OFF + first, count)
        ends.append(
            remote(b.pert.at[STEPS, rows], b.prev_ends.at[rows], b.ends_send.at[i], b.ends_recv.at[i], next_dev)
        )
    dual = []
    for i in range(2):
        down = ~even if i == 0 else even
        src, dst = jnp.where(down, ROWS - 8, 0), jnp.where(down, -8, ROWS)
        sem = jnp.where(down, 0, 1)
        dual.append(
            remote(
                b.dual.at[STEPS, pl.ds(OFF + src, 8)],
                b.dual.at[STEPS, pl.ds(OFF + dst, 8)],
                b.dual_send.at[sem],
                b.dual_recv.at[sem],
                (tm, jnp.where(down, below, above)),
            )
        )

    def dual_arrived(lower):
        rows = b.dual.at[STEPS, pl.ds(OFF + jnp.where(lower, ROWS, -8), 8)]
        sem = jnp.where(lower, 1, 0)
        remote(rows, rows, b.dual_send.at[sem], b.dual_recv.at[sem], up_dev).wait_recv()

    b.forth[...] = order_of(b.forth.shape, True)
    load[1].wait()
    load[0].wait()
    interleave([b.dir_in, b.base_in], b.forth, [b.pert.at[0], b.state.at[0]], [None, SLOPE])
    pl.semaphore_wait(barrier, 4)
    for copy in halo[:2] + back[:1] + halo[2:4] + back[1:] + halo[4:]:
        copy.start()

    def strip(k, low, high, sides, most):
        first_low = low - 1 if sides <= 0 else low + 1
        first_high = high + 1 if sides >= 0 else high - 1
        forward_first(k, b, first_low, first_high - first_low + 1, most, base=k < STEPS - 1)
        forward_second(k, b, low, high - low + 1, most, base=k < STEPS - 1)

    for k in range(STEPS):
        reach = 2 * (STEPS - 1 - k)
        strip(k, 14 - reach, 17 + reach, 0, 32)
    ends[0].start()
    for k in range(STEPS):
        reach = 2 * (STEPS - 1 - k)
        strip(k, 10 - reach, 13 - reach, -1, 32)
        strip(k, 18 + reach, 21 + reach, 1, 32)
    ends[1].start()
    ends[2].start()
    for k in range(STEPS):
        reach = 2 * (STEPS - 1 - k)
        strip(k, 8 - reach, 9 - reach, -1, 32)
        strip(k, 22 + reach, 23 + reach, 1, 32)
    ends[3].start()
    ends[4].start()

    b.back[...] = order_of(b.back.shape, False)
    for copy in halo[:4]:
        copy.wait()
    for k in range(STEPS):
        strip(k, -6 + 2 * k, 1 + 2 * k, -1, 8)
        strip(k, 30 - 2 * k, 37 - 2 * k, 1, 8)
    ends[5].start()
    ends[6].start()

    def residual(first, count):
        rows = pl.ds(OFF + first, count)
        b.dual[STEPS, rows] = b.pert[STEPS, rows] * SCALE - b.next_rows[rows]

    for side in range(2):
        back[side].wait()
        residual(back_row(side), 8)
        dual[side].start()
    for copy in halo[4:]:
        copy.wait()
    for k in range(STEPS):
        last = k == STEPS - 1
        forward_first(k, b, -15 + 2 * k, 8, 8, base=not last, tangent=False)
        forward_first(k, b, 39 - 2 * k, 8, 8, base=not last, tangent=False)
        if not last:
            forward_second(k, b, -14 + 2 * k, 8, 8, tangent=False)
            forward_second(k, b, 38 - 2 * k, 8, 8, tangent=False)

    load[2].wait()
    load[3].wait()
    held = b.levels[...]
    coarse = jnp.zeros(held.shape, jnp.float32)
    for level in range(4):
        coarse = coarse + jnp.where(held == level, b.table[level], 0.0)
    entry = lax.broadcasted_iota(jnp.int32, (8, CHUNKS), 0)
    chunk = lax.broadcasted_iota(jnp.int32, (8, CHUNKS), 1)
    quarter = lax.broadcasted_iota(jnp.int32, (8, LANES), 1) // 32
    for t in range(4):
        value = jnp.zeros((8, LANES), jnp.float32)
        for a in range(4):
            own = jnp.where(chunk == 4 * entry + a, coarse[t : t + 1], 0.0)
            value = value + jnp.where(quarter == a, jnp.sum(own, axis=1, keepdims=True), 0.0)
        b.damp[t] = value

    def turned(first, count):
        return jnp.where(lower_first, first, ROWS - count - first)

    for i in (2, 3):
        back[i].wait()
        residual(back_row(i), 4)
    dual_arrived(lower_first)
    for k in range(STEPS - 1, -1, -1):
        adjoint_first(k, b, turned(27 - 2 * k, 6 + 4 * k), 6 + 4 * k, 32)
        adjoint_second(k, b, turned(28 - 2 * k, 4 + 4 * k), 4 + 4 * k, 32)
    back[4].wait()
    residual(*BACK[4])
    for k in range(STEPS - 1, -1, -1):
        adjoint_first(k, b, turned(7 - 2 * k, 20), 20, 32)
        adjoint_second(k, b, turned(8 - 2 * k, 20), 20, 32)

    def finish(tiles_done):
        parts = [[] for _ in range(4)]
        for t in tiles_done:
            scaled = 1.0 + jnp.concatenate([b.damp[t]] * 4, 0)
            for i in range(8):
                r = OFF + 8 * t + i
                value = (b.dual[0, r] - b.prev_ends[r]) * SCALE + scaled * b.pert[0, r]
                for q in range(4):
                    parts[q].append(value[8 * q : 8 * q + 8])
        out = permute([jnp.concatenate(part, 0) for part in parts], b.back[...])
        for j, t in enumerate(tiles_done):
            for i in range(8):
                for a in range(4):
                    value = out[64 * j + 8 * i : 64 * j + 8 * i + 8, a * LANES : (a + 1) * LANES]
                    product[t, pl.ds(a * 8 + i, 8, 32), :] = value

    dual_arrived(~lower_first)
    for copy in dual:
        copy.wait_send()
    for k in range(STEPS - 1, -1, -1):
        adjoint_first(k, b, turned(-2 * k - 1, 8), 8, 8)
        adjoint_second(k, b, turned(-2 * k, 8), 8, 8)
    for copy in ends[:5]:
        copy.wait()
    finish((1, 2))
    for copy in ends[5:]:
        copy.wait()
    finish((0, 3))


def as_tiles(shard):
    split = shard.reshape(ROWS // 8, 8, CHUNKS, LANES)
    return split.transpose(0, 2, 1, 3).reshape(ROWS // 8, 8 * CHUNKS, LANES)


def solution(mesh):
    segments, slabs = mesh.shape["tm"], mesh.shape["space"]

    def shards(base_start, direction, damp_levels, damp_table):
        any_spec = pl.BlockSpec(memory_space=pl.ANY)
        result = pl.pallas_call(
            functools.partial(kernel, segments, slabs),
            out_shape=tiles(4),
            in_specs=[any_spec] * 4,
            out_specs=pl.BlockSpec(memory_space=pltpu.VMEM),
            scratch_shapes=list(SCRATCH.values()),
            compiler_params=pltpu.CompilerParams(
                collective_id=0, has_side_effects=True, vmem_limit_bytes=56 * 2**20
            ),
        )(as_tiles(base_start), as_tiles(direction), damp_levels, damp_table)
        split = result.reshape(ROWS // 8, CHUNKS, 8, LANES).transpose(0, 2, 1, 3)
        return split.reshape(1, ROWS, COLS)

    in_specs = (P("tm", "space", None), P("tm", "space", None), P("space", None), P())
    out_specs = P("tm", "space", None)
    return jax.shard_map(shards, mesh=mesh, in_specs=in_specs, out_specs=out_specs, check_vma=False)
```
